512 devices in a mesh: dp: 64 (over z_hi, y, core), tensor: 8 (over x, z_lo).
Axes of the slice: x: 4, y: 8, z: 8 (z_hi: 4, z_lo: 2; z = z_hi * 2 + z_lo), core: 2. Of those that a mesh axis runs over, the one named last changes fastest.
Arguments:
- section_input: bfloat16 [2, 8192, 5120], P(None, ('dp', 'tensor')), may hold values from -6 to 6
- w_query: bfloat16 [5120, 8192], P('dp', 'tensor'), may hold values from -0.078125 to 0.078125
- w_kv: bfloat16 [5120, 2, 1024], P(None, None, 'tensor'), may hold values from -0.078125 to 0.078125
- doc_lengths: int32 [64, 2, 4], P('dp'), may hold values from 1 to 64, 128 in all within a row
- d_context: bfloat16 [2, 8192, 8192], P(None, 'dp', 'tensor'), may hold values from -6 to 6
Outputs:
- context: bfloat16 [2, 8192, 8192], P(None, 'dp', 'tensor')
- input_grad: bfloat16 [2, 8192, 5120], P(None, ('dp', 'tensor'))
The draws below stay inside these ranges and needn't reach their ends.
All inputs are finite; a program needn't handle non-finite values.
Results may differ from the reference program's by a relative error of at most 0.019.
Values may be sent and summed in bfloat16 or wider, within the bound.
A program may use at most 64 MiB of HBM per device.

```python
import math
import jax
import jax.numpy as jnp
import numpy as np
from jax import lax

D = 5120
HD = 128
GROUP = 8
MICRO = 2
DOCS = 4
TOK_MB = 128
KVH = 8
HQ = 64
TOKENS = 8192
N_DP = 64
N_TENSOR = 8


def draw_section_input(key, part):
    key = jax.random.fold_in(key, 7)
    first = jax.random.fold_in(key, 0)
    values = jnp.clip(jax.random.normal(first, (MICRO, TOKENS, D), jnp.float32), -6.0, 6.0)
    return values.astype(jnp.bfloat16)


def levels(own_key, dims, cuts, least, top_value):
    def one(position, parts):
        heights = jax.random.uniform(jax.random.fold_in(jax.random.fold_in(own_key, 6), position), (parts,), jnp.float32, least / len(cuts), top_value / len(cuts))
        return jnp.repeat(jnp.exp(heights), dims[position] // parts).reshape((-1,) + (1,) * (len(dims) - position - 1))

    factor_of = one(*cuts[0])
    for cut in cuts[1:]:
        factor_of = factor_of * one(*cut)
    return factor_of


def split_up(amount, total, most, slope):
    weights = [(1 << 20) // math.isqrt(rank ** slope) + 1 for rank in range(2, amount + 1)]
    rest, counts = total - most - (amount - 1), [1] * (amount - 1)
    while rest > 0:
        free = [i for i in range(amount - 1) if counts[i] < most]
        mass, left = sum([weights[i] for i in free]), rest
        for i in free:
            extra = min(most - counts[i], max(1, left * weights[i] // mass), rest)
            counts[i] = counts[i] + extra
            rest = rest - extra
    return np.array([most] + counts)


def ragged_sizes(stream_key, number_of, total, most, lean):
    if number_of == 2:
        one = jax.random.randint(stream_key, (), max(1, total - most), min(most, total - 1) + 1)
        return jnp.stack([one, total - one])
    tallies = jnp.asarray(split_up(number_of, total, most, lean), jnp.int32)
    couples = (number_of - 1) // 2
    donor, taker = tallies[1:1 + 2 * couples:2], tallies[2:2 + 2 * couples:2]
    margin = jnp.minimum(donor - 1, most - taker)
    moved = jax.random.randint(jax.random.fold_in(stream_key, 1), (couples,), 0, 1 << 20) % (margin + 1)
    tallies = tallies.at[1:1 + 2 * couples:2].set(donor - moved).at[2:2 + 2 * couples:2].set(taker + moved)
    return tallies[jax.random.permutation(jax.random.fold_in(stream_key, 2), number_of)]


def bell_draw(own_key, dims, deviation, limit, cuts=(), held_as=jnp.bfloat16):
    values = jax.random.normal(own_key, dims, jnp.float32) * deviation
    if len(cuts) > 0:
        values = levels(own_key, dims, cuts, -0.22, 0.18) * values
    return jnp.clip(values, min=-limit, max=limit).astype(held_as)


def setup_inputs(seed: int = 0) -> dict:
    arg_keys = jax.random.split(jax.random.key(seed), 6)
    section_input = draw_section_input(jax.random.fold_in(arg_keys[5], 71), 0)
    w_query = bell_draw(arg_keys[1], (D, HQ * HD), D ** -0.5, 0.078125, ((0, 64), (1, 8)))
    w_kv = bell_draw(arg_keys[2], (D, 2, KVH * HD), D ** -0.5, 0.078125, ((2, 8),))
    doc_lengths = jax.vmap(lambda own: ragged_sizes(own, DOCS, TOK_MB, TOK_MB // 2, 2))(jax.random.split(arg_keys[3], N_DP * MICRO)).reshape((N_DP, MICRO, DOCS)).astype(jnp.int32)
    d_context = bell_draw(arg_keys[4], (MICRO, TOKENS, HQ * HD), 1.0, 6.0, ((1, 64), (2, 8)))
    return {"section_input": section_input, "w_query": w_query, "w_kv": w_kv, "doc_lengths": doc_lengths, "d_context": d_context}


ROPE_BASE = 1000000.0

def tables(lengths, size, width):
    place = jnp.arange(size, dtype=jnp.int32)
    ends = jnp.cumsum(lengths).astype(jnp.int32)
    after = place[:, None] >= ends[None, :]
    docnum = lax.optimization_barrier(jnp.sum(after.astype(jnp.int32), axis=1)).astype(jnp.int32)
    begin = lax.optimization_barrier(jnp.sum(jnp.where(after, lengths[None, :], 0), axis=1)).astype(jnp.int32)
    offset = (place - begin).astype(jnp.float32)
    half = width // 2
    freq = ROPE_BASE ** (-jnp.arange(half, dtype=jnp.float32) / half)
    angle = offset[:, None] * freq[None, :]
    cosine = jnp.concatenate([jnp.cos(angle), jnp.cos(angle)], axis=1)
    sine = jnp.concatenate([jnp.sin(angle), jnp.sin(angle)], axis=1)
    allowed = (docnum[:, None] == docnum[None, :]) & (place[None, :] <= place[:, None])
    return (cosine, sine, allowed)

def turn(values, cosine, sine):
    half = values.shape[-1] // 2
    rotated = jnp.concatenate([-values[..., half:], values[..., :half]], axis=-1)
    return values * cosine + rotated * sine

def attend(q_raw, k_raw, v_raw, grad_out, lengths):
    size = q_raw.shape[0]
    width = k_raw.shape[1]
    group = q_raw.shape[1] // width
    cosine, sine, allowed = tables(lengths, size, width)
    query = turn(q_raw.reshape(size, group, width), cosine[:, None, :], sine[:, None, :]).astype(jnp.bfloat16)
    key_rows = turn(k_raw, cosine, sine).astype(jnp.bfloat16)
    value_rows = v_raw.astype(jnp.bfloat16)
    scale = 1.0 / math.sqrt(width)
    scores = jnp.einsum('sgd,td->gst', query.astype(jnp.float32), key_rows.astype(jnp.float32)) * scale
    scores = jnp.where(allowed[None], scores, -1e+30)
    top = lax.optimization_barrier(jnp.max(scores, axis=-1, keepdims=True))
    expo = jnp.exp(scores - top)
    probs = expo / lax.optimization_barrier(jnp.sum(expo, axis=-1, keepdims=True))
    weights = probs.astype(jnp.bfloat16)
    context = jnp.einsum('gst,td->sgd', weights.astype(jnp.float32), value_rows.astype(jnp.float32)).astype(jnp.bfloat16)
    upstream = grad_out.reshape(size, group, width).astype(jnp.float32)
    d_weights = jnp.einsum('sgd,td->gst', upstream, value_rows.astype(jnp.float32))
    d_value = jnp.einsum('gst,sgd->td', weights.astype(jnp.float32), upstream).astype(jnp.bfloat16)
    d_scores = (probs * (d_weights - lax.optimization_barrier(jnp.sum(probs * d_weights, axis=-1, keepdims=True))) * scale).astype(jnp.bfloat16)
    d_query = turn(jnp.einsum('gst,td->sgd', d_scores.astype(jnp.float32), key_rows.astype(jnp.float32)), cosine[:, None, :], -sine[:, None, :]).astype(jnp.bfloat16)
    d_key = turn(jnp.einsum('gst,sgd->td', d_scores.astype(jnp.float32), query.astype(jnp.float32)), cosine, -sine).astype(jnp.bfloat16)
    return (context.reshape(size, group * width), d_query.reshape(size, group * width), d_key, d_value)

def reference(section_input, w_query, w_kv, doc_lengths, d_context):
    rows_all = section_input.reshape(MICRO, N_DP, TOK_MB, D).transpose(1, 0, 2, 3)
    grads_all = d_context.reshape(MICRO, N_DP, TOK_MB, HQ * HD).transpose(1, 0, 2, 3)
    span = GROUP * HD

    def replica(packed):
        rows, lengths, upstream = packed
        contexts = []
        totals = []
        for index in range(MICRO):
            total = jnp.zeros((TOK_MB, D), jnp.float32)
            pieces = []
            for shard in range(N_TENSOR):
                wq = w_query[:, shard * span:(shard + 1) * span]
                wk = w_kv[:, 0, shard * HD:(shard + 1) * HD]
                wv = w_kv[:, 1, shard * HD:(shard + 1) * HD]
                q_raw = jnp.dot(rows[index], wq, preferred_element_type=jnp.float32)
                k_raw = jnp.dot(rows[index], wk, preferred_element_type=jnp.float32)
                v_raw = jnp.dot(rows[index], wv, preferred_element_type=jnp.float32)
                ctx, d_query, d_key, d_value = attend(q_raw, k_raw, v_raw, upstream[index][:, shard * span:(shard + 1) * span], lengths[index])
                partial_value = jnp.dot(d_query, wq.T, preferred_element_type=jnp.float32)
                partial_value = partial_value + jnp.dot(d_key, wk.T, preferred_element_type=jnp.float32)
                partial_value = partial_value + jnp.dot(d_value, wv.T, preferred_element_type=jnp.float32)
                total = total + lax.optimization_barrier(partial_value.astype(jnp.bfloat16)).astype(jnp.float32)
                pieces.append(ctx)
            contexts.append(jnp.concatenate(pieces, axis=1))
            totals.append(total.astype(jnp.bfloat16))
        return (jnp.stack(contexts), jnp.stack(totals))
    ctxs, grads = lax.map(replica, (rows_all, doc_lengths, grads_all))
    context = ctxs.transpose(1, 0, 2, 3).reshape(MICRO, N_DP * TOK_MB, HQ * HD)
    input_grad = grads.transpose(1, 0, 2, 3).reshape(MICRO, N_DP * TOK_MB, D)
    return (context, input_grad)
```

```python
import math

import jax
import jax.numpy as jnp
import numpy as np
from jax import lax
from jax.experimental import pallas as pl
from jax.experimental.pallas import tpu as pltpu
from jax.sharding import PartitionSpec as P

ROPE_BASE = 1000000.0
MESH = pl.DeviceIdType.MESH
F32 = jnp.float32
BF16 = jnp.bfloat16

NZ, NY, NX = 4, 8, 4
T = NX * 2
MICRO = 2
LOC = 16
SEQ = T * LOC
D = 5120
HD = 128
GROUP = 8
QC = GROUP * HD
ROWS = 80
PH = 2
PC = QC // PH
HPP = GROUP // PH
NB = 5
DB = D // NB
SCALE = 1.0 / math.sqrt(HD)


def nt(a, b):
    return lax.dot_general(a, b, (((1,), (1,)), ((), ())), preferred_element_type=F32)


def tn(a, b):
    return lax.dot_general(a, b, (((0,), (0,)), ((), ())), preferred_element_type=F32)


def nn(a, b):
    return jnp.dot(a, b, preferred_element_type=F32)


def body(
    x_hbm, w_hbm, kv_hbm, len_ref, dctx_hbm, freq_ref,
    ctx_hbm, grad_hbm,
    xbuf, wbuf, kvi, kvf, wkv, dctx, cos_t, sin_t, mask_t, qraw, kvraw, ctx, dqb, dkvb,
    kbuf, vbuf, dkacc, dvacc, acc, pbuf, accin, accout, fin_m, fin_p, zout, zin, keep, outb,
    loc_sem, wz_s, wz_r, wy_s, wy_r, wc_s, wc_r, x_s, x_r, r_s, r_r,
):
    dp = lax.axis_index("dp")
    t = lax.axis_index("tensor")
    zh, y, c = dp // 16, (dp // 2) % 8, dp % 2
    x, zl = t // 2, t % 2

    def dev(dzh=0, dy=0, dc=0, dx=0, dzl=0):
        a = ((zh + dzh) % NZ) * 16 + ((y + dy) % NY) * 2 + (c + dc) % 2
        return (a, ((x + dx) % NX) * 2 + (zl + dzl) % 2)

    core = dev(dc=1)
    yp, ym = dev(dy=1), dev(dy=-1 + NY)
    zp, zm = dev(dzh=1), dev(dzh=-1 + NZ)
    xp, xm = dev(dx=1), dev(dx=-1 + NX)
    zpair = dev(dzl=1)

    def rows_of(dzh, dy, dc=0):
        a = ((zh + dzh) % NZ) * 16 + ((y + dy) % NY) * 2 + (c + dc) % 2
        return pl.multiple_of(a * ROWS, 16)

    own = rows_of(0, 0)
    load_w = pltpu.make_async_copy(w_hbm, wbuf.at[pl.ds(own, ROWS), :], loc_sem.at[0])
    load_x = pltpu.make_async_copy(x_hbm, xbuf.at[t], loc_sem.at[1])
    load_kv = pltpu.make_async_copy(kv_hbm, kvi, loc_sem.at[2])
    load_d = pltpu.make_async_copy(dctx_hbm, dctx, loc_sem.at[3])
    for cp in (load_w, load_x, load_kv, load_d):
        cp.start()

    bar = pltpu.get_barrier_semaphore()
    for d in (core, yp, ym, zp, zm, xp, xm, zpair):
        pl.semaphore_signal(bar, 1, device_id=d, device_id_type=MESH)
    pl.semaphore_wait(bar, 8)

    def send(src, dst, ss, rs, d):
        pltpu.make_async_remote_copy(
            src_ref=src, dst_ref=dst, send_sem=ss, recv_sem=rs, device_id=d, device_id_type=MESH
        ).start()

    def same(ref, ss, rs, d):
        send(ref, ref, ss, rs, d)

    def got(ref, sem):
        pltpu.make_async_copy(ref, ref, sem).wait()

    def wchunk(dzh, dy, p, part=None):
        col, width = p * PC, PC
        if part is not None:
            width = PC // 2
            col = col + part * width
        return wbuf.at[pl.ds(rows_of(dzh, dy), ROWS), pl.ds(col, width)]

    zoff = (0, NZ - 1, 1, 2)

    def start_z(p):
        ref = wchunk(0, 0, p)
        same(ref, wz_s.at[p], wz_r.at[p, 0], zp)
        same(ref, wz_s.at[p], wz_r.at[p, 1], zm)

    def start_y(p, j):
        ref = wchunk(zoff[j], 0, p)
        same(ref, wy_s.at[p], wy_r.at[p, j, 0, 0], yp)
        same(ref, wy_s.at[p], wy_r.at[p, j, 0, 1], ym)
        same(ref, wc_s.at[p], wc_r.at[p], core)

    def step_z1(p):
        got(wchunk(NZ - 1, 0, p), wz_r.at[p, 0])
        same(wchunk(NZ - 1, 0, p, 0), wz_s.at[p], wz_r.at[p, 2], zp)
        got(wchunk(1, 0, p), wz_r.at[p, 1])
        same(wchunk(1, 0, p, 1), wz_s.at[p], wz_r.at[p, 3], zm)

    def step_z2(p):
        got(wchunk(2, 0, p, 0), wz_r.at[p, 2])
        got(wchunk(2, 0, p, 1), wz_r.at[p, 3])

    def step_y(p, j, h):
        o = zoff[j]
        if h < 4:
            lo, hi = wchunk(o, NY - h, p), wchunk(o, h, p)
            got(lo, wy_r.at[p, j, h - 1, 0])
            if h < 3:
                same(lo, wy_s.at[p], wy_r.at[p, j, h, 0], yp)
            else:
                same(wchunk(o, NY - h, p, 0), wy_s.at[p], wy_r.at[p, j, h, 0], yp)
            same(lo, wc_s.at[p], wc_r.at[p], core)
            got(hi, wy_r.at[p, j, h - 1, 1])
            if h < 3:
                same(hi, wy_s.at[p], wy_r.at[p, j, h, 1], ym)
            else:
                same(wchunk(o, h, p, 1), wy_s.at[p], wy_r.at[p, j, h, 1], ym)
            same(hi, wc_s.at[p], wc_r.at[p], core)
        else:
            got(wchunk(o, 4, p, 0), wy_r.at[p, j, 3, 0])
            got(wchunk(o, 4, p, 1), wy_r.at[p, j, 3, 1])
            same(wchunk(o, 4, p), wc_s.at[p], wc_r.at[p], core)

    def core_done(p):
        ref = wbuf.at[pl.ds(0, D // 2), pl.ds(p * PC, PC)]
        got(ref, wc_r.at[p])

    def xrow(dx, dzl):
        return ((x + dx) % NX) * 2 + (zl + dzl) % 2

    def start_x(b):
        r = xbuf.at[xrow(0, b)]
        same(r, x_s.at[1 + b], x_r.at[1 + 4 * b], xp)
        same(r, x_s.at[1 + b], x_r.at[2 + 4 * b], xm)

    def start_xz():
        same(xbuf.at[t], x_s.at[0], x_r.at[0], zpair)

    def step_xz():
        got(xbuf.at[xrow(0, 1)], x_r.at[0])
        start_x(1)

    def step_x1(b):
        r = xrow(NX - 1, b)
        got(xbuf.at[r], x_r.at[1 + 4 * b])
        same(xbuf.at[r, 0], x_s.at[1 + b], x_r.at[3 + 4 * b], xp)
        r = xrow(1, b)
        got(xbuf.at[r], x_r.at[2 + 4 * b])
        same(xbuf.at[r, 1], x_s.at[1 + b], x_r.at[4 + 4 * b], xm)

    def step_x2(b):
        r = xrow(2, b)
        got(xbuf.at[r, 0], x_r.at[3 + 4 * b])
        got(xbuf.at[r, 1], x_r.at[4 + 4 * b])

    def make_tables():
        lanes = lax.broadcasted_iota(jnp.int32, (SEQ, HD), 1)
        place = lax.broadcasted_iota(jnp.int32, (SEQ, HD), 0)
        sign = jnp.where(lanes < HD // 2, -1.0, 1.0).astype(F32)
        freq = freq_ref[0:1, :]
        for m in range(MICRO):
            end = jnp.int32(0)
            begin = jnp.zeros((SEQ, HD), jnp.int32)
            doc_s = jnp.zeros((SEQ, HD), jnp.int32)
            doc_t = jnp.zeros((SEQ, HD), jnp.int32)
            for k in range(4):
                length = len_ref[0, m, k]
                end = end + length
                after = place >= end
                begin = begin + jnp.where(after, length, 0)
                doc_s = doc_s + after.astype(jnp.int32)
                doc_t = doc_t + (lanes >= end).astype(jnp.int32)
            angle = (place - begin).astype(F32) * freq
            cos_t[m] = jnp.cos(angle)
            sin_t[m] = jnp.sin(angle) * sign
            mask_t[m] = jnp.where((doc_s == doc_t) & (lanes <= place), 1.0, 0.0).astype(F32)

    def split_kv(i):
        n = D // 8

        def one(k, _):
            kvf[...] = kvi[pl.ds(pl.multiple_of(k * 2 * n, 16), 2 * n), :].astype(F32)
            at = pl.ds(pl.multiple_of(k * n, 16), n)
            wkv[at, 0:HD] = kvf[pl.ds(0, n, stride=2), :].astype(BF16)
            wkv[at, HD:2 * HD] = kvf[pl.ds(1, n, stride=2), :].astype(BF16)
            return 0

        lax.fori_loop(2 * i, 2 * i + 2, one, 0)

    def turn(v, m, back=False):
        rolled = pltpu.roll(v, HD // 2, 1) * sin_t[m]
        return v * cos_t[m] - rolled if back else v * cos_t[m] + rolled

    KB = 1024

    def kv_mm():
        total = jnp.zeros((T * MICRO * LOC, 2 * HD), F32)
        for k in range(D // KB):
            rows = xbuf[:, :, :, k * KB:(k + 1) * KB].reshape(T * MICRO * LOC, KB)
            total = total + nn(rows, wkv[k * KB:(k + 1) * KB, :])
        kvraw[...] = total.reshape(T, MICRO, LOC, 2 * HD)
        for m in range(MICRO):
            kr = kvraw[:, m, :, 0:HD].reshape(SEQ, HD)
            kbuf[m] = turn(kr, m).astype(BF16)
            vbuf[m] = kvraw[:, m, :, HD:2 * HD].reshape(SEQ, HD).astype(BF16)

    def q_mm(p, k):
        rows = xbuf[:, :, :, k * KB:(k + 1) * KB].reshape(T * MICRO * LOC, KB)
        part = nn(rows, wbuf[k * KB:(k + 1) * KB, p * PC:(p + 1) * PC])
        part = part.reshape(T, MICRO, LOC, PC)
        if k == 0:
            qraw[...] = part
        else:
            qraw[...] += part

    def attend(p, m):
        key, val = kbuf[m], vbuf[m]
        queries, ups = [], []
        for h in range(HPP):
            qr = qraw[:, m, :, h * HD:(h + 1) * HD].reshape(SEQ, HD)
            queries.append(turn(qr, m).astype(BF16))
            g = p * HPP + h
            ups.append(dctx[m, :, g * HD:(g + 1) * HD])
        query = jnp.concatenate(queries, axis=0)
        up = jnp.concatenate(ups, axis=0)
        mask = jnp.concatenate([mask_t[m]] * HPP, axis=0) > 0.5
        s = jnp.where(mask, nt(query, key) * SCALE, -1e30)
        e = jnp.exp(s - jnp.max(s, axis=1, keepdims=True))
        probs = e / jnp.sum(e, axis=1, keepdims=True)
        w = probs.astype(BF16)
        out = nn(w, val).astype(BF16)
        dw = nt(up, val)
        ds = (probs * (dw - jnp.sum(probs * dw, axis=1, keepdims=True)) * SCALE).astype(BF16)
        dv = tn(w, up)
        dk = tn(ds, query)
        if p == 0:
            dvacc[m] = dv
            dkacc[m] = dk
        else:
            dvacc[m] += dv
            dkacc[m] += dk
        dq = nn(ds, key)
        for h in range(HPP):
            g = p * HPP + h
            at = slice(g * HD, (g + 1) * HD)
            ctx[m, :, at] = out[h * SEQ:(h + 1) * SEQ]
            piece = turn(dq[h * SEQ:(h + 1) * SEQ], m, True).astype(BF16)
            dqb[:, m, :, at] = piece.reshape(T, LOC, HD)
        if p == PH - 1:
            dk = turn(dkacc[m], m, True).astype(BF16)
            dkvb[:, m, :, 0:HD] = dk.reshape(T, LOC, HD)
            dkvb[:, m, :, HD:2 * HD] = dvacc[m].astype(BF16).reshape(T, LOC, HD)

    def back_first(k):
        at = slice(k * DB, (k + 1) * DB)
        lhs = dqb[:, :, :, 0:PC].reshape(T * MICRO * LOC, PC)
        acc[:, at] = nt(lhs, wbuf[at, 0:PC])

    def back_last(k):
        at = slice(k * DB, (k + 1) * DB)
        lhs = dqb[:, :, :, PC:].reshape(T * MICRO * LOC, PC)
        lkv = dkvb[...].reshape(T * MICRO * LOC, 2 * HD)
        total = acc[:, at] + nt(lhs, wbuf[at, PC:]) + nt(lkv, wkv[at, :])
        pbuf[:, at] = total.astype(BF16)

    XR = 2 * MICRO * LOC

    def xrows(dx):
        return pl.ds(pl.multiple_of(((x + dx) % NX) * XR, 16), XR)

    def halves(b):
        half = DB // 2
        return pl.ds(b * DB, half), pl.ds(b * DB + half, half)

    def rs_start(b):
        ca, cb = halves(b)
        send(pbuf.at[xrows(2), ca], accin.at[:, ca], r_s.at[0], r_r.at[b, 0], xp)
        send(pbuf.at[xrows(2), cb], accin.at[:, cb], r_s.at[0], r_r.at[b, 1], xm)
        send(pbuf.at[xrows(1), cb], fin_m.at[:, cb], r_s.at[0], r_r.at[b, 2], xp)
        send(pbuf.at[xrows(NX - 1), ca], fin_p.at[:, ca], r_s.at[0], r_r.at[b, 3], xm)

    def rs_add(b):
        ca, cb = halves(b)
        got(accin.at[:, ca], r_r.at[b, 0])
        accout[:, ca] = (accin[:, ca].astype(F32) + pbuf[xrows(1), ca].astype(F32)).astype(BF16)
        send(accout.at[:, ca], fin_m.at[:, ca], r_s.at[0], r_r.at[b, 4], xp)
        got(accin.at[:, cb], r_r.at[b, 1])
        accout[:, cb] = (accin[:, cb].astype(F32) + pbuf[xrows(NX - 1), cb].astype(F32)).astype(BF16)
        send(accout.at[:, cb], fin_p.at[:, cb], r_s.at[0], r_r.at[b, 5], xm)

    ZR = MICRO * LOC

    def rs_join(b):
        ca, cb = halves(b)
        full = pl.ds(b * DB, DB)
        got(fin_m.at[:, cb], r_r.at[b, 2])
        got(fin_p.at[:, ca], r_r.at[b, 3])
        got(fin_m.at[:, ca], r_r.at[b, 4])
        got(fin_p.at[:, cb], r_r.at[b, 5])
        mine = pl.ds(pl.multiple_of(zl * ZR, 16), ZR)
        theirs = pl.ds(pl.multiple_of((1 - zl) * ZR, 16), ZR)

        def total(rows, which):
            return (
                fin_m[which, full].astype(F32) + fin_p[which, full].astype(F32)
                + pbuf[rows, full].astype(F32)
            )

        base = ((x % NX) * 2) * ZR
        zout[:, full] = total(pl.ds(pl.multiple_of(base + (1 - zl) * ZR, 16), ZR), theirs).astype(BF16)
        send(zout.at[:, full], zin.at[:, full], r_s.at[1], r_r.at[b, 6], zpair)
        keep[:, full] = total(pl.ds(pl.multiple_of(base + zl * ZR, 16), ZR), mine)

    def rs_last(b):
        full = pl.ds(b * DB, DB)
        got(zin.at[:, full], r_r.at[b, 6])
        res = (keep[:, full] + zin[:, full].astype(F32)).astype(BF16)
        outb[:, :, full] = res.reshape(MICRO, LOC, DB)

    load_w.wait()
    start_y(0, 0)
    start_z(0)
    load_x.wait()
    start_x(0)
    start_xz()
    make_tables()
    load_kv.wait()
    step_y(0, 0, 1)
    start_y(1, 0)
    step_z1(0)
    start_y(0, 1)
    start_y(0, 2)
    step_y(0, 0, 2)
    step_x1(0)
    step_z2(0)
    start_y(0, 3)
    start_z(1)
    split_kv(0)
    step_y(0, 1, 1)
    step_y(0, 2, 1)
    step_xz()
    step_y(0, 0, 3)
    step_y(0, 3, 1)
    split_kv(1)
    step_y(0, 1, 2)
    step_y(0, 2, 2)
    step_x2(0)
    step_y(0, 0, 4)
    step_z1(1)
    step_y(0, 3, 2)
    split_kv(2)
    step_y(1, 0, 1)
    step_x1(1)
    step_y(0, 1, 3)
    step_y(0, 2, 3)
    start_y(1, 1)
    start_y(1, 2)
    step_z2(1)
    step_y(0, 3, 3)
    start_y(1, 3)
    split_kv(3)
    step_x2(1)
    step_y(0, 1, 4)
    step_y(0, 2, 4)
    step_y(0, 3, 4)
    core_done(0)
    load_d.wait()

    pieces = [kv_mm]
    pieces += [lambda k=k: q_mm(0, k) for k in range(D // KB)]
    pieces += [lambda m=m: attend(0, m) for m in range(MICRO)]
    pieces += [lambda k=k: back_first(k) for k in range(NB)]
    steps = [(0, 2), (1, 1), (2, 1), (3, 1), (0, 3), (1, 2), (2, 2), (3, 2), (0, 4), (1, 3), (2, 3), (3, 3), (1, 4), (2, 4), (3, 4)]
    while steps or pieces:
        if steps:
            j, h = steps.pop(0)
            step_y(1, j, h)
        if pieces:
            pieces.pop(0)()
    core_done(1)
    for k in range(D // KB):
        q_mm(1, k)
    for m in range(MICRO):
        attend(1, m)
    put_ctx = pltpu.make_async_copy(ctx, ctx_hbm, loc_sem.at[4])
    put_ctx.start()
    for b in range(NB):
        back_last(b)
        rs_start(b)
    for b in range(NB):
        rs_add(b)
        if b > 0:
            rs_join(b - 1)
        if b > 1:
            rs_last(b - 2)
    rs_join(NB - 1)
    rs_last(NB - 2)
    rs_last(NB - 1)
    put_grad = pltpu.make_async_copy(outb, grad_hbm, loc_sem.at[5])
    put_grad.start()

    def sent(n_rows, n_cols, sem):
        got(wbuf.at[pl.ds(0, n_rows), pl.ds(0, n_cols)], sem)

    for p in range(PH):
        sent(3 * ROWS, PC, wz_s.at[p])
        sent(28 * ROWS, PC, wy_s.at[p])
        sent(32 * ROWS, PC, wc_s.at[p])
    got(xbuf.at[0], x_s.at[0])
    for b in range(2):
        got(xbuf.at[pl.ds(0, 3)], x_s.at[1 + b])
    got(pbuf.at[pl.ds(0, 3 * XR), :], r_s.at[0])
    got(zout, r_s.at[1])
    put_ctx.wait()
    put_grad.wait()


def run(x_in, w_in, kv_in, lens, d_in):
    half = HD // 2
    freq = (ROPE_BASE ** (-np.arange(half, dtype=np.float32) / np.float32(half))).astype(np.float32)
    freq = jnp.asarray(np.broadcast_to(np.concatenate([freq, freq])[None], (8, HD)))
    kv2 = kv_in.reshape(2 * D, HD)
    anyspec = pl.BlockSpec(memory_space=pl.ANY)
    dma, vm = pltpu.SemaphoreType.DMA, pltpu.VMEM
    scratch = [
        vm((T, MICRO, LOC, D), BF16),
        vm((D, QC), BF16),
        vm((2 * D, HD), BF16),
        vm((2 * D // 8, HD), F32),
        vm((D, 2 * HD), BF16),
        vm((MICRO, SEQ, QC), BF16),
        vm((MICRO, SEQ, HD), F32),
        vm((MICRO, SEQ, HD), F32),
        vm((MICRO, SEQ, HD), F32),
        vm((T, MICRO, LOC, PC), F32),
        vm((T, MICRO, LOC, 2 * HD), F32),
        vm((MICRO, SEQ, QC), BF16),
        vm((T, MICRO, LOC, QC), BF16),
        vm((T, MICRO, LOC, 2 * HD), BF16),
        vm((MICRO, SEQ, HD), BF16),
        vm((MICRO, SEQ, HD), BF16),
        vm((MICRO, SEQ, HD), F32),
        vm((MICRO, SEQ, HD), F32),
        vm((T * MICRO * LOC, D), F32),
        vm((T * MICRO * LOC, D), BF16),
        vm((2 * MICRO * LOC, D), BF16),
        vm((2 * MICRO * LOC, D), BF16),
        vm((2 * MICRO * LOC, D), BF16),
        vm((2 * MICRO * LOC, D), BF16),
        vm((MICRO * LOC, D), BF16),
        vm((MICRO * LOC, D), BF16),
        vm((MICRO * LOC, D), F32),
        vm((MICRO, LOC, D), BF16),
        dma((6,)),
        dma((PH,)),
        dma((PH, 4)),
        dma((PH,)),
        dma((PH, 4, 4, 2)),
        dma((PH,)),
        dma((PH,)),
        dma((3,)),
        dma((9,)),
        dma((2,)),
        dma((NB, 7)),
    ]
    return pl.pallas_call(
        body,
        name="layer",
        out_shape=(
            jax.ShapeDtypeStruct((MICRO, SEQ, QC), BF16),
            jax.ShapeDtypeStruct((MICRO, LOC, D), BF16),
        ),
        in_specs=[
            anyspec, anyspec, anyspec, pl.BlockSpec(memory_space=pltpu.SMEM), anyspec,
            pl.BlockSpec(memory_space=pltpu.VMEM),
        ],
        out_specs=(anyspec, anyspec),
        scratch_shapes=scratch,
        compiler_params=pltpu.CompilerParams(
            collective_id=0, has_side_effects=True, vmem_limit_bytes=56 << 20
        ),
        cost_estimate=pl.CostEstimate(flops=7_500_000_000, bytes_accessed=5_000_000, transcendentals=1_000_000),
    )(x_in, w_in, kv2, lens, d_in, freq)


def solution(mesh):
    return jax.shard_map(
        run,
        mesh=mesh,
        in_specs=(
            P(None, ("dp", "tensor"), None),
            P("dp", "tensor"),
            P(None, None, "tensor"),
            P("dp", None, None),
            P(None, "dp", "tensor"),
        ),
        out_specs=(P(None, "dp", "tensor"), P(None, ("dp", "tensor"), None)),
        check_vma=False,
    )
```

```python
import math

import jax
import jax.numpy as jnp
from jax import lax
from jax.experimental import pallas as pl
from jax.experimental.pallas import tpu as pltpu
from jax.sharding import PartitionSpec as P

ROPE_BASE = 1000000.0
MESH = pl.DeviceIdType.MESH
F32 = jnp.float32
BF16 = jnp.bfloat16

NZ, NY, NX = 4, 8, 4
T = NX * 2
MICRO = 2
LOC = 16
SEQ = T * LOC
D = 5120
HD = 128
GROUP = 8
QC = GROUP * HD
ROWS = 80
PW = (384, 256, 128)
QW = (128, 128, 0)
PC = tuple(u + v for u, v in zip(PW, QW))
PH = len(PW)
HP = tuple(v // HD for v in PC)
COL = tuple(sum(PC[:i]) for i in range(PH + 1))
NB = 8
DB = D // NB
KB = D // NZ
SCALE = 1.0 / math.sqrt(HD)
ZFIRST = (1, 2, 3)
ORDER = (
    ("qo", 0), ("xo",), ("zo", 0), ("xp",), ("yo", 0), ("tab",), ("qy", 0, 1), ("qo", 1), ("yo", 1),
    ("kvs", 0), ("ys", 0, 0, 1), ("kvs", 1), ("qy", 0, 2), ("yo", 2), ("z1", 0), ("yz", 0, 1), ("yz", 0, 2),
    ("qy", 1, 1), ("ys", 1, 0, 1), ("kvs", 2), ("kvs", 3), ("qy", 0, 3), ("ys", 0, 0, 2), ("zo", 1),
    ("x1", 0), ("ys", 2, 0, 1), ("xz",), ("z2", 0), ("yz", 0, 3), ("ys", 0, 1, 1), ("ys", 0, 2, 1),
    ("qy", 1, 2), ("ys", 1, 0, 2), ("qy", 0, 4), ("qz", 0, 0), ("z1", 1), ("ys", 0, 0, 3), ("x2", 0),
    ("ys", 2, 0, 2), ("ys", 0, 3, 1), ("ys", 0, 1, 2), ("ys", 0, 2, 2), ("qy", 1, 3), ("ys", 1, 0, 3),
    ("ys", 0, 0, 4), ("zo", 2), ("ys", 2, 0, 3), ("x1", 1), ("ys", 0, 3, 2), ("qz", 0, 1), ("ys", 0, 1, 3),
    ("z2", 1), ("z1", 2), ("yz", 1, 1), ("ys", 0, 2, 3), ("qy", 1, 4), ("qz", 1, 0), ("ys", 1, 0, 4),
    ("ys", 2, 0, 4), ("yz", 1, 2), ("x2", 1), ("kvm",), ("ys", 0, 1, 4), ("ys", 0, 3, 3), ("yz", 1, 3),
    ("ys", 1, 1, 1), ("qz", 0, 2), ("ys", 0, 2, 4), ("z2", 2), ("yz", 2, 1), ("yz", 2, 2), ("ys", 1, 2, 1),
    ("ys", 0, 3, 4), ("yz", 2, 3), ("ys", 1, 3, 1), ("cd", 0), ("qm", 0, 0), ("ys", 1, 1, 2), ("qm", 0, 1),
    ("ys", 2, 1, 1), ("ys", 2, 2, 1), ("qm", 0, 2), ("qm", 0, 3), ("ys", 1, 2, 2), ("at", 0, 0),
    ("ys", 2, 3, 1), ("ys", 1, 3, 2), ("at", 0, 1), ("qz", 1, 1), ("ys", 1, 1, 3), ("ys", 2, 1, 2),
    ("ys", 2, 2, 2), ("bf", 0, 0), ("bf", 0, 1), ("ys", 1, 2, 3), ("bf", 0, 2), ("ys", 2, 3, 2), ("bf", 0, 3),
    ("bf", 0, 4), ("ys", 1, 3, 3), ("bf", 0, 5), ("ys", 1, 1, 4), ("bf", 0, 6), ("ys", 2, 1, 3), ("bf", 0, 7),
    ("ys", 2, 2, 3), ("ys", 1, 2, 4), ("ys", 2, 3, 3), ("ys", 1, 3, 4), ("ys", 2, 1, 4), ("qz", 1, 2),
    ("ys", 2, 2, 4), ("ys", 2, 3, 4), ("cd", 1), ("qm", 1, 0), ("qm", 1, 1), ("qm", 1, 2), ("cd", 2),
    ("qm", 1, 3), ("at", 1, 0), ("at", 1, 1), ("bf", 1, 0), ("bf", 1, 1), ("bf", 1, 2), ("bf", 1, 3),
    ("bf", 1, 4), ("bf", 1, 5), ("bf", 1, 6), ("bf", 1, 7), ("qm", 2, 0), ("qm", 2, 1), ("qm", 2, 2),
    ("qm", 2, 3), ("at", 2, 0), ("at", 2, 1), ("bl", 0), ("bl", 1), ("bl", 2), ("bl", 3), ("bl", 4),
    ("bl", 5), ("bl", 6), ("bl", 7), ("rb", 0), ("rb", 4), ("zj", 1), ("rb", 5), ("rb", 6), ("zj", 2),
    ("rb", 7), ("rj", 0), ("rj", 4), ("zj", 3), ("rb", 1), ("rj", 5), ("rl", 0), ("rj", 6), ("rl", 4),
    ("rb", 2), ("rj", 7), ("rl", 5), ("rb", 3), ("rl", 6), ("rj", 1), ("rj", 2), ("rl", 7), ("rj", 3),
)


def nt(a, b):
    return lax.dot_general(a, b, (((1,), (1,)), ((), ())), preferred_element_type=F32)


def tn(a, b):
    return lax.dot_general(a, b, (((0,), (0,)), ((), ())), preferred_element_type=F32)


def nn(a, b):
    return jnp.dot(a, b, preferred_element_type=F32)


def body(
    x_hbm, w_hbm, kv_hbm, len_ref, dctx_hbm,
    ctx_hbm, grad_hbm,
    xbuf, wb0, wb1, wb2, kvi, kvf, wkv, dctx, cos_t, sin_t, mask_t, qraw, kvraw, ctx, dqb, dkvb,
    kbuf, vbuf, dkacc, dvacc, acc, pbuf, accin, accout, fin_m, fin_p, zout, zin, zinb, keep, outb,
    loc_sem, wz_s, wz_r, wy_s, wy_r, qy_s, qy_r, qz_s, qz_r, wc_s, wc_r, x_s, x_r, r_s, r_r,
):
    wbuf = (wb0, wb1, wb2)
    dp = lax.axis_index("dp")
    t = lax.axis_index("tensor")
    zh, y, c = dp // 16, (dp // 2) % 8, dp % 2
    x, zl = t // 2, t % 2

    def dev(dzh=0, dy=0, dc=0, dx=0, dzl=0):
        a = ((zh + dzh) % NZ) * 16 + ((y + dy) % NY) * 2 + (c + dc) % 2
        return (a, ((x + dx) % NX) * 2 + (zl + dzl) % 2)

    core = dev(dc=1)
    yp, ym = dev(dy=1), dev(dy=-1 + NY)
    zp, zm = dev(dzh=1), dev(dzh=-1 + NZ)
    xr, xm = dev(dx=1), dev(dx=-1 + NX)
    zpair = dev(dzl=1)

    load_w = [
        pltpu.make_async_copy(
            w_hbm.at[:, pl.ds(COL[p], PC[p])], wbuf[p].at[zh, y, c], loc_sem.at[6 + p]
        )
        for p in range(PH)
    ]
    load_x = pltpu.make_async_copy(x_hbm, xbuf.at[t], loc_sem.at[1])
    load_kv = pltpu.make_async_copy(kv_hbm, kvi, loc_sem.at[2])
    load_d = pltpu.make_async_copy(dctx_hbm, dctx, loc_sem.at[3])
    for cp in (*load_w, load_x, load_kv, load_d):
        cp.start()

    bar = pltpu.get_barrier_semaphore()
    for d in (core, yp, ym, zp, zm, xr, xm, zpair):
        pl.semaphore_signal(bar, 1, device_id=d, device_id_type=MESH)
    pl.semaphore_wait(bar, 8)

    def send(src, dst, ss, rs, d):
        pltpu.make_async_remote_copy(
            src_ref=src, dst_ref=dst, send_sem=ss, recv_sem=rs, device_id=d, device_id_type=MESH
        ).start()

    def same(ref, ss, rs, d):
        send(ref, ref, ss, rs, d)

    def got(ref, sem):
        pltpu.make_async_copy(ref, ref, sem).wait()

    def zi(dzh):
        return (zh + dzh + NZ) % NZ

    def yi(dy):
        return (y + dy + NY) % NY

    def wchunk(p, dzh, dy, rows=(0, ROWS)):
        return wbuf[p].at[zi(dzh), yi(dy), c, pl.ds(rows[0], rows[1]), pl.ds(0, PW[p])]

    def qchunk(p, dy, rows=(0, ROWS)):
        return wbuf[p].at[zh, yi(dy), c, pl.ds(rows[0], rows[1]), pl.ds(PW[p], QW[p])]

    def qblock(p, dzh, half=None):
        ys = pl.ds(0, NY) if half is None else pl.ds(half * (NY // 2), NY // 2)
        return wbuf[p].at[zi(dzh), ys, c, :, pl.ds(PW[p], QW[p])]

    def cut(n):
        first = 48 if n % 2 == 0 else 32
        return (0, first), (first, ROWS - first)

    zoff = (0, -1, 1, 2)

    def yo(p):
        yz(p, 0)

    def yz(p, j):
        ref = wchunk(p, zoff[j], 0)
        same(ref, wy_s.at[p], wy_r.at[p, j, 0, 0], yp)
        same(ref, wy_s.at[p], wy_r.at[p, j, 0, 1], ym)
        same(ref, wc_s.at[p], wc_r.at[p], core)

    def zo(p):
        ref = wchunk(p, 0, 0)
        same(ref, wz_s.at[p], wz_r.at[p, 0], zp)
        same(ref, wz_s.at[p], wz_r.at[p, 1], zm)

    def z1(p):
        one, two = cut(p)
        got(wchunk(p, -1, 0), wz_r.at[p, 0])
        same(wchunk(p, -1, 0, one), wz_s.at[p], wz_r.at[p, 2], zp)
        got(wchunk(p, 1, 0), wz_r.at[p, 1])
        same(wchunk(p, 1, 0, two), wz_s.at[p], wz_r.at[p, 3], zm)

    def z2(p):
        one, two = cut(p)
        got(wchunk(p, 2, 0, one), wz_r.at[p, 2])
        got(wchunk(p, 2, 0, two), wz_r.at[p, 3])

    def ys(p, j, h):
        o = zoff[j]
        one, two = cut(p + j)
        if h < 4:
            lo, hi = wchunk(p, o, -h), wchunk(p, o, h)
            far = h == 3
            got(lo, wy_r.at[p, j, h - 1, 0])
            same(wchunk(p, o, -h, one) if far else lo, wy_s.at[p], wy_r.at[p, j, h, 0], yp)
            same(lo, wc_s.at[p], wc_r.at[p], core)
            got(hi, wy_r.at[p, j, h - 1, 1])
            same(wchunk(p, o, h, two) if far else hi, wy_s.at[p], wy_r.at[p, j, h, 1], ym)
            same(hi, wc_s.at[p], wc_r.at[p], core)
        else:
            got(wchunk(p, o, 4, one), wy_r.at[p, j, 3, 0])
            got(wchunk(p, o, 4, two), wy_r.at[p, j, 3, 1])
            same(wchunk(p, o, 4), wc_s.at[p], wc_r.at[p], core)

    def qo(p):
        same(qchunk(p, 0), qy_s.at[p], qy_r.at[p, 0, 0], yp)
        same(qchunk(p, 0), qy_s.at[p], qy_r.at[p, 0, 1], ym)

    def qy(p, h):
        one, two = cut(p)
        if h < 4:
            far = h == 3
            got(qchunk(p, -h), qy_r.at[p, h - 1, 0])
            same(qchunk(p, -h, one) if far else qchunk(p, -h), qy_s.at[p], qy_r.at[p, h, 0], yp)
            got(qchunk(p, h), qy_r.at[p, h - 1, 1])
            same(qchunk(p, h, two) if far else qchunk(p, h), qy_s.at[p], qy_r.at[p, h, 1], ym)
        else:
            got(qchunk(p, 4, one), qy_r.at[p, 3, 0])
            got(qchunk(p, 4, two), qy_r.at[p, 3, 1])

    def qz(p, step):
        if step == 0:
            same(qblock(p, 0), qz_s.at[p], qz_r.at[p, 0], zp)
            same(qblock(p, 0), qz_s.at[p], qz_r.at[p, 1], zm)
            same(qblock(p, 0), wc_s.at[p], wc_r.at[p], core)
        elif step == 1:
            got(qblock(p, -1), qz_r.at[p, 0])
            same(qblock(p, -1, 0), qz_s.at[p], qz_r.at[p, 2], zp)
            same(qblock(p, -1), wc_s.at[p], wc_r.at[p], core)
            got(qblock(p, 1), qz_r.at[p, 1])
            same(qblock(p, 1, 1), qz_s.at[p], qz_r.at[p, 3], zm)
            same(qblock(p, 1), wc_s.at[p], wc_r.at[p], core)
        else:
            got(qblock(p, 2, 0), qz_r.at[p, 2])
            got(qblock(p, 2, 1), qz_r.at[p, 3])
            same(qblock(p, 2), wc_s.at[p], wc_r.at[p], core)

    def cd(p):
        got(wbuf[p].at[:, :, 0], wc_r.at[p])

    def xrow(dx, dzl):
        return ((x + dx) % NX) * 2 + (zl + dzl) % 2

    def start_x(b):
        r = xbuf.at[xrow(0, b)]
        same(r, x_s.at[1 + b], x_r.at[1 + 4 * b], xr)
        same(r, x_s.at[1 + b], x_r.at[2 + 4 * b], xm)

    def xp():
        same(xbuf.at[t], x_s.at[0], x_r.at[0], zpair)

    def xz():
        got(xbuf.at[xrow(0, 1)], x_r.at[0])
        start_x(1)

    def x1(b):
        r = xrow(NX - 1, b)
        got(xbuf.at[r], x_r.at[1 + 4 * b])
        same(xbuf.at[r, 0], x_s.at[1 + b], x_r.at[3 + 4 * b], xr)
        r = xrow(1, b)
        got(xbuf.at[r], x_r.at[2 + 4 * b])
        same(xbuf.at[r, 1], x_s.at[1 + b], x_r.at[4 + 4 * b], xm)

    def x2(b):
        r = xrow(2, b)
        got(xbuf.at[r, 0], x_r.at[3 + 4 * b])
        got(xbuf.at[r, 1], x_r.at[4 + 4 * b])

    def tab():
        lanes = lax.broadcasted_iota(jnp.int32, (SEQ, HD), 1)
        place = lax.broadcasted_iota(jnp.int32, (SEQ, HD), 0)
        sign = jnp.where(lanes < HD // 2, -1.0, 1.0).astype(F32)
        index = jnp.where(lanes < HD // 2, lanes, lanes - HD // 2).astype(F32)
        freq = jnp.exp(index * (-math.log(ROPE_BASE) / (HD // 2)))
        for m in range(MICRO):
            end = jnp.int32(0)
            begin = jnp.zeros((SEQ, HD), jnp.int32)
            doc_s = jnp.zeros((SEQ, HD), jnp.int32)
            doc_t = jnp.zeros((SEQ, HD), jnp.int32)
            for k in range(4):
                length = len_ref[0, m, k]
                end = end + length
                after = place >= end
                begin = begin + jnp.where(after, length, 0)
                doc_s = doc_s + after.astype(jnp.int32)
                doc_t = doc_t + (lanes >= end).astype(jnp.int32)
            angle = (place - begin).astype(F32) * freq
            cos_t[m] = jnp.cos(angle)
            sin_t[m] = jnp.sin(angle) * sign
            mask_t[m] = jnp.where((doc_s == doc_t) & (lanes <= place), 1.0, 0.0).astype(F32)

    def kvs(i):
        n = D // 8

        def one(k, _):
            kvf[...] = kvi[pl.ds(pl.multiple_of(k * 2 * n, 16), 2 * n), :].astype(F32)
            at = pl.ds(pl.multiple_of(k * n, 16), n)
            wkv[at, 0:HD] = kvf[pl.ds(0, n, stride=2), :].astype(BF16)
            wkv[at, HD:2 * HD] = kvf[pl.ds(1, n, stride=2), :].astype(BF16)
            return 0

        lax.fori_loop(2 * i, 2 * i + 2, one, 0)

    def turn(v, m, back=False):
        rolled = pltpu.roll(v, HD // 2, 1) * sin_t[m]
        return v * cos_t[m] - rolled if back else v * cos_t[m] + rolled

    def kvm():
        total = jnp.zeros((T * MICRO * LOC, 2 * HD), F32)
        for k in range(D // KB):
            rows = xbuf[:, :, :, k * KB:(k + 1) * KB].reshape(T * MICRO * LOC, KB)
            total = total + nn(rows, wkv[k * KB:(k + 1) * KB, :])
        kvraw[...] = total.reshape(T, MICRO, LOC, 2 * HD)
        for m in range(MICRO):
            kr = kvraw[:, m, :, 0:HD].reshape(SEQ, HD)
            kbuf[m] = turn(kr, m).astype(BF16)
            vbuf[m] = kvraw[:, m, :, HD:2 * HD].reshape(SEQ, HD).astype(BF16)

    def qm(p, k):
        n = PC[p]
        rows = xbuf[:, :, :, k * KB:(k + 1) * KB].reshape(T * MICRO * LOC, KB)
        part = nn(rows, wbuf[p][k].reshape(KB, n)).reshape(T, MICRO, LOC, n)
        if k == 0:
            qraw[:, :, :, 0:n] = part
        else:
            qraw[:, :, :, 0:n] += part

    def at(p, m):
        key, val = kbuf[m], vbuf[m]
        queries, ups = [], []
        for h in range(HP[p]):
            qr = qraw[:, m, :, h * HD:(h + 1) * HD].reshape(SEQ, HD)
            queries.append(turn(qr, m).astype(BF16))
            g = COL[p] // HD + h
            ups.append(dctx[m, :, g * HD:(g + 1) * HD])
        query = jnp.concatenate(queries, axis=0)
        up = jnp.concatenate(ups, axis=0)
        mask = jnp.concatenate([mask_t[m]] * HP[p], axis=0) > 0.5
        s = jnp.where(mask, nt(query, key) * SCALE, -1e30)
        e = jnp.exp(s - jnp.max(s, axis=1, keepdims=True))
        probs = e / jnp.sum(e, axis=1, keepdims=True)
        w = probs.astype(BF16)
        out = nn(w, val).astype(BF16)
        dw = nt(up, val)
        ds = (probs * (dw - jnp.sum(probs * dw, axis=1, keepdims=True)) * SCALE).astype(BF16)
        dv = tn(w, up)
        dk = tn(ds, query)
        if p == 0:
            dvacc[m] = dv
            dkacc[m] = dk
        else:
            dvacc[m] += dv
            dkacc[m] += dk
        dq = nn(ds, key)
        for h in range(HP[p]):
            g = COL[p] // HD + h
            cols = slice(g * HD, (g + 1) * HD)
            ctx[m, :, cols] = out[h * SEQ:(h + 1) * SEQ]
            piece = turn(dq[h * SEQ:(h + 1) * SEQ], m, True).astype(BF16)
            dqb[:, m, :, cols] = piece.reshape(T, LOC, HD)
        if p == PH - 1:
            dk = turn(dkacc[m], m, True).astype(BF16)
            dkvb[:, m, :, 0:HD] = dk.reshape(T, LOC, HD)
            dkvb[:, m, :, HD:2 * HD] = dvacc[m].astype(BF16).reshape(T, LOC, HD)

    def back(p, k):
        lhs = dqb[:, :, :, COL[p]:COL[p + 1]].reshape(T * MICRO * LOC, PC[p])
        half = NY // 2
        lo = (k % 2) * half
        return nt(lhs, wbuf[p][k // 2, lo:lo + half].reshape(DB, PC[p]))

    def bf(p, k):
        cols = slice(k * DB, (k + 1) * DB)
        if p == 0:
            acc[:, cols] = back(p, k)
        else:
            acc[:, cols] += back(p, k)

    ZR = MICRO * LOC

    def xi(dx):
        return (x + dx + NX) % NX

    def at_cols(b):
        return pl.ds(b * DB, DB)

    def part(b, dx, half):
        if b in ZFIRST:
            return pbuf.at[xi(dx), zl, pl.ds(half * LOC, LOC), at_cols(b)]
        return pbuf.at[xi(dx), half, :, at_cols(b)]

    def slot(buf, b, half):
        if b in ZFIRST:
            return buf.at[0, pl.ds(half * LOC, LOC), at_cols(b)]
        return buf.at[half, :, at_cols(b)]

    def ring(b):
        send(part(b, 2, 0), slot(accin, b, 0), r_s.at[b, 0], r_r.at[b, 0], xr)
        send(part(b, 2, 1), slot(accin, b, 1), r_s.at[b, 0], r_r.at[b, 1], xm)
        send(part(b, 1, 1), slot(fin_m, b, 1), r_s.at[b, 0], r_r.at[b, 2], xr)
        send(part(b, -1, 0), slot(fin_p, b, 0), r_s.at[b, 0], r_r.at[b, 3], xm)

    def bl(b):
        cols = slice(b * DB, (b + 1) * DB)
        lkv = dkvb[...].reshape(T * MICRO * LOC, 2 * HD)
        total = acc[:, cols] + back(PH - 1, b) + nt(lkv, wkv[cols, :])
        pbuf[:, :, :, cols] = total.astype(BF16).reshape(NX, 2, ZR, DB)
        if b in ZFIRST:
            send(
                pbuf.at[:, 1 - zl, :, at_cols(b)], zinb.at[:, :, at_cols(b)],
                r_s.at[b, 1], r_r.at[b, 6], zpair,
            )
        else:
            ring(b)

    def zj(b):
        cols = slice(b * DB, (b + 1) * DB)
        got(zinb.at[:, :, at_cols(b)], r_r.at[b, 6])
        mine = pbuf[:, zl, :, cols].astype(F32) + zinb[:, :, cols].astype(F32)
        pbuf[:, zl, :, cols] = mine.astype(BF16)
        ring(b)

    def rb(b):
        for half, dx, to, fin, k in ((0, 1, xr, fin_m, 0), (1, -1, xm, fin_p, 1)):
            got(slot(accin, b, half), r_r.at[b, k])
            both = slot(accin, b, half)[...].astype(F32) + part(b, dx, half)[...].astype(F32)
            slot(accout, b, half)[...] = both.astype(BF16)
            send(slot(accout, b, half), slot(fin, b, half), r_s.at[b, 0], r_r.at[b, 4 + k], to)

    def store(b, res):
        outb[:, :, b * DB:(b + 1) * DB] = res.astype(BF16).reshape(MICRO, LOC, DB)
        at = (slice(None), slice(None), at_cols(b))
        pltpu.make_async_copy(outb.at[at], grad_hbm.at[at], loc_sem.at[5]).start()

    def rj(b):
        cols = slice(b * DB, (b + 1) * DB)
        got(slot(fin_m, b, 1), r_r.at[b, 2])
        got(slot(fin_p, b, 0), r_r.at[b, 3])
        got(slot(fin_m, b, 0), r_r.at[b, 4])
        got(slot(fin_p, b, 1), r_r.at[b, 5])

        def total(w, own):
            return (
                fin_m[w, :, cols].astype(F32) + fin_p[w, :, cols].astype(F32)
                + pbuf[x, own, :, cols].astype(F32)
            )

        if b in ZFIRST:
            store(b, total(0, zl))
        else:
            zout[:, cols] = total(1 - zl, 1 - zl).astype(BF16)
            send(zout.at[:, at_cols(b)], zin.at[:, at_cols(b)], r_s.at[b, 1], r_r.at[b, 6], zpair)
            keep[:, cols] = total(zl, zl)

    def rl(b):
        cols = slice(b * DB, (b + 1) * DB)
        got(zin.at[:, at_cols(b)], r_r.at[b, 6])
        store(b, keep[:, cols] + zin[:, cols].astype(F32))

    for cp in load_w:
        cp.wait()
    load_x.wait()
    run_of = dict(
        yo=yo, yz=yz, zo=zo, z1=z1, z2=z2, ys=ys, qo=qo, qy=qy, qz=qz, cd=cd,
        xo=lambda: start_x(0), xp=xp, xz=xz, x1=x1, x2=x2,
        tab=tab, kvs=kvs, kvm=kvm, qm=qm, at=at, bf=bf, bl=bl, zj=zj, rb=rb, rj=rj, rl=rl,
    )
    put_ctx = pltpu.make_async_copy(ctx, ctx_hbm, loc_sem.at[4])
    for name, *args in ORDER:
        if (name, *args) == ("kvs", 0):
            load_kv.wait()
        if (name, *args) == ("at", 0, 0):
            load_d.wait()
        run_of[name](*args)
        if (name, *args) == ("at", PH - 1, MICRO - 1):
            put_ctx.start()

    for p in range(PH):
        got(wbuf[p].at[pl.ds(0, 3), 0, 0, :, pl.ds(0, PW[p])], wz_s.at[p])
        got(wbuf[p].at[:, pl.ds(0, 7), 0, :, pl.ds(0, PW[p])], wy_s.at[p])
        got(wbuf[p].at[:, :, 0], wc_s.at[p])
        if QW[p]:
            got(wbuf[p].at[0, pl.ds(0, 7), 0, :, pl.ds(PW[p], QW[p])], qy_s.at[p])
            got(wbuf[p].at[pl.ds(0, 3), :, 0, :, pl.ds(PW[p], QW[p])], qz_s.at[p])
    got(xbuf.at[0], x_s.at[0])
    for b in range(2):
        got(xbuf.at[pl.ds(0, 3)], x_s.at[1 + b])
    for b in range(NB):
        if b in ZFIRST:
            got(pbuf.at[pl.ds(0, 3), 0, :, at_cols(b)], r_s.at[b, 0])
            got(pbuf.at[:, 0, :, at_cols(b)], r_s.at[b, 1])
        else:
            got(pbuf.at[pl.ds(0, 3), :, :, at_cols(b)], r_s.at[b, 0])
            got(pbuf.at[0, 0, :, at_cols(b)], r_s.at[b, 1])
    put_ctx.wait()
    got(outb, loc_sem.at[5])


def run(x_in, w_in, kv_in, lens, d_in):
    kv2 = kv_in.reshape(2 * D, HD)
    anyspec = pl.BlockSpec(memory_space=pl.ANY)
    dma, vm = pltpu.SemaphoreType.DMA, pltpu.VMEM
    scratch = [
        vm((T, MICRO, LOC, D), BF16),
        *[vm((NZ, NY, 2, ROWS, PC[p]), BF16) for p in range(PH)],
        vm((2 * D, HD), BF16),
        vm((2 * D // 8, HD), F32),
        vm((D, 2 * HD), BF16),
        vm((MICRO, SEQ, QC), BF16),
        vm((MICRO, SEQ, HD), F32),
        vm((MICRO, SEQ, HD), F32),
        vm((MICRO, SEQ, HD), F32),
        vm((T, MICRO, LOC, PC[0]), F32),
        vm((T, MICRO, LOC, 2 * HD), F32),
        vm((MICRO, SEQ, QC), BF16),
        vm((T, MICRO, LOC, QC), BF16),
        vm((T, MICRO, LOC, 2 * HD), BF16),
        vm((MICRO, SEQ, HD), BF16),
        vm((MICRO, SEQ, HD), BF16),
        vm((MICRO, SEQ, HD), F32),
        vm((MICRO, SEQ, HD), F32),
        vm((T * MICRO * LOC, D), F32),
        vm((NX, 2, MICRO * LOC, D), BF16),
        *[vm((2, MICRO * LOC, D), BF16) for _ in range(4)],
        vm((MICRO * LOC, D), BF16),
        vm((MICRO * LOC, D), BF16),
        vm((NX, MICRO * LOC, D), BF16),
        vm((MICRO * LOC, D), F32),
        vm((MICRO, LOC, D), BF16),
        dma((9,)),
        dma((PH,)),
        dma((PH, 4)),
        dma((PH,)),
        dma((PH, 4, 4, 2)),
        dma((PH,)),
        dma((PH, 4, 2)),
        dma((PH,)),
        dma((PH, 4)),
        dma((PH,)),
        dma((PH,)),
        dma((3,)),
        dma((9,)),
        dma((NB, 2)),
        dma((NB, 7)),
    ]
    return pl.pallas_call(
        body,
        name="layer",
        out_shape=(
            jax.ShapeDtypeStruct((MICRO, SEQ, QC), BF16),
            jax.ShapeDtypeStruct((MICRO, LOC, D), BF16),
        ),
        in_specs=[
            anyspec, anyspec, anyspec, pl.BlockSpec(memory_space=pltpu.SMEM), anyspec,
        ],
        out_specs=(anyspec, anyspec),
        scratch_shapes=scratch,
        compiler_params=pltpu.CompilerParams(
            collective_id=0, has_side_effects=True, vmem_limit_bytes=56 << 20
        ),
        cost_estimate=pl.CostEstimate(flops=7_500_000_000, bytes_accessed=5_000_000, transcendentals=1_000_000),
    )(x_in, w_in, kv2, lens, d_in)


def solution(mesh):
    return jax.shard_map(
        run,
        mesh=mesh,
        in_specs=(
            P(None, ("dp", "tensor"), None),
            P("dp", "tensor"),
            P(None, None, "tensor"),
            P("dp", None, None),
            P(None, "dp", "tensor"),
        ),
        out_specs=(P(None, "dp", "tensor"), P(None, ("dp", "tensor"), None)),
        check_vma=False,
    )
```
